256 devices in a mesh: replica: 16 (over x_lo, y, core), tensor: 16 (over x_hi, z).
Axes of the slice: x: 4 (x_hi: 2, x_lo: 2; x = x_hi * 2 + x_lo), y: 4, z: 8, core: 2. Of those that a mesh axis runs over, the one named last changes fastest.
Arguments:
- params: bfloat16 [16, 4096, 4096], P('replica', None, 'tensor'), may hold values from -6 to 6
- anchor: float32 [512, 4096], P(None, 'tensor'), may hold values from -6 to 6
- momentum: float32 [512, 4096], P(None, 'tensor'), may hold values from -4 to 4
- tokens: bfloat16 [16, 1, 2048, 4096], P('replica', None, 'tensor'), may hold values from -6 to 6
- fragment: int32 [1], replicated, may hold values from 0 to 7
Outputs:
- params_out: bfloat16 [16, 4096, 4096], P('replica', None, 'tensor')
- momentum_out: float32 [512, 4096], P(None, 'tensor')
- anchor_out: float32 [512, 4096], P(None, 'tensor')
The draws below stay inside these ranges and needn't reach their ends.
Inputs may be any that keep to these rules, and one draw needn't show every extreme that they name: `fragment`: the index of one of the 8 fragments.
All inputs are finite; a program needn't handle non-finite values.
Results may differ from the reference program's by a relative error of at most 0.0034.
Values may be sent and summed in bfloat16 or wider, within the bound.
A program may use at most 64 MiB of HBM per device.

```python
import math
import jax
import jax.numpy as jnp
from jax import lax

D = 4096
STEPS = 1
FRAGMENTS = 8
TOK_REP = 2048
N_REPLICA = 16


def shard_levels(stream_key, extent, shards, smallest, largest):
    def one(axis_at, shards_of):
        heights = jax.random.uniform(jax.random.fold_in(jax.random.fold_in(stream_key, 6), axis_at), (shards_of,), jnp.float32, smallest / len(shards), largest / len(shards))
        return jnp.repeat(jnp.exp(heights), extent[axis_at] // shards_of).reshape((-1,) + (1,) * (len(extent) - axis_at - 1))

    factor_of = one(*shards[0])
    for cut in shards[1:]:
        factor_of = factor_of * one(*cut)
    return factor_of


def centred(key, extent, deviation, most, split=(), kind=jnp.bfloat16):
    values = deviation * jax.random.normal(key, extent, jnp.float32)
    if split:
        values = values * shard_levels(key, extent, split, -0.22, 0.18)
    return jnp.clip(values, -most, most).astype(kind)


def setup_inputs(seed: int = 0) -> dict:
    key_list = jax.random.split(jax.random.key(seed), 6)
    params = centred(key_list[0], (N_REPLICA, D, D), 1.0, 6.0, ((0, 16), (2, 16)))
    anchor = centred(key_list[1], (D // FRAGMENTS, D), 1.0, 6.0, ((1, 16),), jnp.float32)
    momentum = centred(key_list[2], (D // FRAGMENTS, D), 0.5, 4.0, ((1, 16),), jnp.float32)
    tokens = centred(key_list[3], (N_REPLICA, STEPS, TOK_REP, D), 1.0, 6.0, ((0, 16), (2, 16)))
    fragment = jax.random.randint(key_list[4], (1,), 0, FRAGMENTS).astype(jnp.int32)
    return {"params": params, "anchor": anchor, "momentum": momentum, "tokens": tokens, "fragment": fragment}


inner_rate = 128.0
outer_rate = 0.7
nesterov_mu = 0.9

def inner_round(weight, batch_rows):
    inv_root = 1.0 / math.sqrt(D)
    outputs = jnp.dot(batch_rows, weight, preferred_element_type=jnp.float32) * inv_root
    residual = (outputs - batch_rows.astype(jnp.float32)).astype(jnp.bfloat16)
    gradient = jnp.dot(batch_rows.T, residual, preferred_element_type=jnp.float32) * (inv_root / TOK_REP)
    return (weight.astype(jnp.float32) - inner_rate * gradient).astype(jnp.bfloat16)

def reference(params, anchor, momentum, tokens, fragment):
    frag_rows = D // FRAGMENTS
    first_row = (fragment[0] * frag_rows).astype(jnp.int32)

    def per_replica(packed):
        weight, batches = packed
        before = weight
        for inner_step in range(STEPS):
            if inner_step == STEPS - 1:
                before = weight
            weight = inner_round(weight, batches[inner_step])
        before_rows = lax.dynamic_slice_in_dim(before, first_row, frag_rows, 0).astype(jnp.float32)
        after_rows = lax.dynamic_slice_in_dim(weight, first_row, frag_rows, 0).astype(jnp.float32)
        return (anchor - before_rows, after_rows - before_rows, weight)
    drifts, lates, finals = lax.map(per_replica, (params, tokens))
    outer_grad = lax.optimization_barrier(jnp.sum(drifts, axis=0)) / N_REPLICA
    momentum_out = nesterov_mu * momentum + outer_grad
    anchor_out = anchor - outer_rate * (outer_grad + nesterov_mu * momentum_out)
    merged = (anchor_out[None] + lates).astype(jnp.bfloat16)
    params_out = lax.dynamic_update_slice_in_dim(finals, merged, first_row, 1)
    return (params_out, momentum_out, anchor_out)
```

```python
import functools
import math

import jax
import jax.numpy as jnp
from jax import lax
from jax.experimental import pallas as pl
from jax.experimental.pallas import tpu as pltpu
from jax.sharding import PartitionSpec as P

FRAGMENTS = 8
CHUNKS = 4
W_PIECES = 8
TILES = 8

inner_rate = 128.0
outer_rate = 0.7
nesterov_mu = 0.9

MESH = pl.DeviceIdType.MESH


def step_kernel(
    nz, total_rows, x_ref, w_ref, o_ref,
    xb, wv, acc, resid, stage,
    own_send, w_send, w_recv, got, ring_send, sib_send, out_send, out_recv,
):
    rows, width = x_ref.shape
    columns = w_ref.shape[1]
    chunk = rows // CHUNKS
    piece = width // W_PIECES
    tile = width // TILES
    inv_root = 1.0 / math.sqrt(width)

    rep = lax.axis_index("replica")
    ten = lax.axis_index("tensor")
    core = lax.rem(rep, 2)
    far = ten // nz
    z = lax.rem(ten, nz)
    ahead = lax.rem(z + 1 - 2 * core + nz, nz)
    behind = lax.rem(z - 1 + 2 * core + nz, nz)
    nxt = (rep, far * nz + ahead)
    prv = (rep, far * nz + behind)
    sibling = (rep + 1 - 2 * core, ten)
    partner = (rep + 1 - 2 * core, (1 - far) * nz + z)
    swapped = core + far == 1
    col_first = pl.multiple_of((core * nz + z) * columns, columns)
    mine = core * rows
    other = (1 - core) * rows

    barrier = pltpu.get_barrier_semaphore()
    for peer in (nxt, prv, sibling):
        pl.semaphore_signal(barrier, inc=1, device_id=peer, device_id_type=MESH)

    @pl.when(swapped)
    def _():
        pl.semaphore_signal(barrier, inc=1, device_id=partner, device_id_type=MESH)
        pl.semaphore_wait(barrier, 4)

    @pl.when(jnp.logical_not(swapped))
    def _():
        pl.semaphore_wait(barrier, 3)

    def remote(src, dst, send, recv, peer):
        return pltpu.make_async_remote_copy(
            src_ref=src, dst_ref=dst, send_sem=send, recv_sem=recv, device_id=peer, device_id_type=MESH
        )

    def x_over(j):
        return remote(
            x_ref.at[pl.ds(j * chunk, chunk)], xb.at[0, pl.ds(other + j * chunk, chunk)],
            own_send.at[j], got.at[0, 0, j], partner,
        )

    def w_over(k):
        return remote(
            w_ref.at[pl.ds(k * piece, piece)], wv.at[pl.ds(k * piece, piece)],
            w_send.at[k], w_recv.at[k], partner,
        )

    def x_here(j):
        return pltpu.make_async_copy(
            x_ref.at[pl.ds(j * chunk, chunk)], xb.at[0, pl.ds(mine + j * chunk, chunk)], got.at[0, 0, j]
        )

    def w_here(k):
        return pltpu.make_async_copy(
            w_ref.at[pl.ds(k * piece, piece)], wv.at[pl.ds(k * piece, piece)], w_recv.at[k]
        )

    @pl.when(swapped)
    def _():
        for j in range(CHUNKS):
            x_over(j).start()
        for k in range(W_PIECES):
            w_over(k).start()

    @pl.when(jnp.logical_not(swapped))
    def _():
        for j in range(CHUNKS):
            x_here(j).start()
        for k in range(W_PIECES):
            w_here(k).start()

    def arrived(s, lane, j):
        place = (mine if lane == 0 else other) + j * chunk
        ref = xb.at[s, pl.ds(place, chunk)]
        pltpu.make_async_copy(ref, ref, got.at[s, lane, j]).wait()

    def ring(s, j):
        place = pl.ds(mine + j * chunk, chunk)
        return remote(xb.at[s, place], xb.at[s + 1, place], ring_send.at[s, j], got.at[s + 1, 0, j], nxt)

    def share(s, j):
        place = pl.ds(mine + j * chunk, chunk)
        return remote(xb.at[s, place], xb.at[s, place], sib_send.at[s, j], got.at[s, 1, j], sibling)

    def pass_on(s, j, onward):
        arrived(s, 0, j)
        if onward:
            ring(s, j).start()
        share(s, j).start()

    def forward(s):
        for j in range(CHUNKS):
            arrived(s, 1, j)
        outputs = jnp.dot(xb[s], wv[...], preferred_element_type=jnp.float32) * inv_root
        target = xb[s, :, pl.ds(col_first, columns)].astype(jnp.float32)
        resid[...] = (outputs - target).astype(jnp.bfloat16)

    def grad_tile(s, t):
        return lax.dot_general(
            xb[s, :, pl.ds(t * tile, tile)], resid[...], (((0,), (0,)), ((), ())),
            preferred_element_type=jnp.float32,
        )

    def backward(s):
        @pl.loop(0, TILES)
        def _(t):
            t = pl.multiple_of(t * tile, tile)
            acc[pl.ds(t, tile), :] += lax.dot_general(
                xb[s, :, pl.ds(t, tile)], resid[...], (((0,), (0,)), ((), ())),
                preferred_element_type=jnp.float32,
            )

    acc[...] = jnp.zeros_like(acc)
    half = nz // 2

    def early(s, carry):
        for j in range(CHUNKS):
            pass_on(s, j, True)
        return carry

    lax.fori_loop(0, half, early, 0)

    for k in range(W_PIECES):
        ref = wv.at[pl.ds(k * piece, piece)]
        pltpu.make_async_copy(ref, ref, w_recv.at[k]).wait()

    def late(s, carry):
        first = 2 * (s - half)
        pass_on(s, 0, True)
        forward(first)
        pass_on(s, 1, True)
        backward(first)
        pass_on(s, 2, True)
        forward(first + 1)
        pass_on(s, 3, True)
        backward(first + 1)
        return carry

    lax.fori_loop(half, nz - 1, late, 0)

    last = nz - 1
    pass_on(last, 0, False)
    forward(last - 1)
    pass_on(last, 1, False)
    backward(last - 1)
    pass_on(last, 2, False)
    pass_on(last, 3, False)
    forward(last)

    def out_over(t):
        place = pl.ds(t * tile, tile)
        return remote(stage.at[place], o_ref.at[place], out_send.at[t], out_recv.at[t], partner)

    def out_here(t):
        place = pl.ds(t * tile, tile)
        return pltpu.make_async_copy(stage.at[place], o_ref.at[place], out_recv.at[t])

    for t in range(TILES):
        place = pl.ds(t * tile, tile)
        gradient = acc[place, :] + grad_tile(last, t)
        scaled = gradient * (inv_root / total_rows)
        stage[place, :] = (wv[place, :].astype(jnp.float32) - inner_rate * scaled).astype(jnp.bfloat16)

        @pl.when(swapped)
        def _():
            out_over(t).start()

        @pl.when(jnp.logical_not(swapped))
        def _():
            out_here(t).start()

    @pl.when(swapped)
    def _():
        for j in range(CHUNKS):
            x_over(j).wait_send()
        for k in range(W_PIECES):
            w_over(k).wait_send()
        for t in range(TILES):
            out_over(t).wait()

    @pl.when(jnp.logical_not(swapped))
    def _():
        for t in range(TILES):
            out_here(t).wait()

    def drain(s, carry):
        for j in range(CHUNKS):
            share(s, j).wait_send()
        return carry

    lax.fori_loop(0, nz, drain, 0)

    def drain_ring(s, carry):
        for j in range(CHUNKS):
            ring(s, j).wait_send()
        return carry

    lax.fori_loop(0, nz - 1, drain_ring, 0)


def inner_step(nz, tokens, weight):
    rows, width = tokens.shape
    columns = weight.shape[1]
    total_rows = rows * 2 * nz
    flops = 4 * total_rows * width * columns
    return pl.pallas_call(
        functools.partial(step_kernel, nz, total_rows),
        out_shape=jax.ShapeDtypeStruct((width, columns), jnp.bfloat16),
        in_specs=[pl.BlockSpec(memory_space=pl.ANY)] * 2,
        out_specs=pl.BlockSpec(memory_space=pl.ANY),
        scratch_shapes=[
            pltpu.VMEM((nz, 2 * rows, width), jnp.bfloat16),
            pltpu.VMEM((width, columns), jnp.bfloat16),
            pltpu.VMEM((width, columns), jnp.float32),
            pltpu.VMEM((2 * rows, columns), jnp.bfloat16),
            pltpu.VMEM((width, columns), jnp.bfloat16),
            pltpu.SemaphoreType.DMA((CHUNKS,)),
            pltpu.SemaphoreType.DMA((W_PIECES,)),
            pltpu.SemaphoreType.DMA((W_PIECES,)),
            pltpu.SemaphoreType.DMA((nz, 2, CHUNKS)),
            pltpu.SemaphoreType.DMA((nz - 1, CHUNKS)),
            pltpu.SemaphoreType.DMA((nz, CHUNKS)),
            pltpu.SemaphoreType.DMA((TILES,)),
            pltpu.SemaphoreType.DMA((TILES,)),
        ],
        cost_estimate=pl.CostEstimate(flops=flops, bytes_accessed=8 << 20, transcendentals=0),
        compiler_params=pltpu.CompilerParams(
            collective_id=0, has_side_effects=True, vmem_limit_bytes=48 << 20
        ),
    )(tokens, weight)


def local(nz, params, anchor, momentum, tokens, fragment):
    weight = params[0]
    width = weight.shape[0]
    frag_rows = width // FRAGMENTS
    first_row = fragment[0] * frag_rows
    before_rows = lax.dynamic_slice_in_dim(weight, first_row, frag_rows, 0).astype(jnp.float32)
    drift = anchor - before_rows
    summed = lax.psum(drift, "replica")
    outer_grad = summed / lax.axis_size("replica")
    momentum_out = nesterov_mu * momentum + outer_grad
    anchor_out = anchor - outer_rate * (outer_grad + nesterov_mu * momentum_out)
    after = inner_step(nz, tokens[0, 0], weight)
    after_rows = lax.dynamic_slice_in_dim(after, first_row, frag_rows, 0).astype(jnp.float32)
    merged = (anchor_out + (after_rows - before_rows)).astype(jnp.bfloat16)
    params_out = lax.dynamic_update_slice_in_dim(after, merged, first_row, 0)
    return (params_out[None], momentum_out, anchor_out)


def solution(mesh):
    return jax.shard_map(
        functools.partial(local, mesh.shape["tensor"] // 2),
        mesh=mesh,
        in_specs=(
            P("replica", None, "tensor"),
            P(None, "tensor"),
            P(None, "tensor"),
            P("replica", None, "tensor", None),
            P(),
        ),
        out_specs=(P("replica", None, "tensor"), P(None, "tensor"), P(None, "tensor")),
        check_vma=False,
    )
```

```python
import functools
import math

import jax
import jax.numpy as jnp
from jax import lax
from jax.experimental import pallas as pl
from jax.experimental.pallas import tpu as pltpu
from jax.sharding import PartitionSpec as P

LATE_ROWS = 16
PARTS = (2, 3, 1, 1)
CHUNKS = len(PARTS)
W_PIECES = 8
TILES = 8

inner_rate = 128.0
outer_rate = 0.7
nesterov_mu = 0.9

MESH = pl.DeviceIdType.MESH


def step_kernel(
    nz, ny, total_rows, frag_ref, x_ref, w_ref, a_ref, m_ref, o_ref, mo_ref, ao_ref,
    xb, xq, wv, home, acc, resid, resid_late, stage, relay, back, fin,
    anchor, momentum, frag_out, frag_in, part, from_x, from_y, grad,
    own_send, w_send, w_recv, got, ring_send, sib_send, out_send, relay_recv, relay_send, back_recv,
    q_own, mate_send, mate_recv, q_send, q_recv, fin_sem, load_sem, store_sem,
    a_send, a_recv, b_send, b_recv, c_send, c_recv, d_send, d_recv, e_send, e_recv, f_send, f_recv,
):
    shard, width = x_ref.shape
    rows = shard - LATE_ROWS
    columns = w_ref.shape[1]
    sizes = [rows * part // 7 for part in PARTS]
    starts = [sum(sizes[:j]) for j in range(CHUNKS)]
    piece = width // W_PIECES
    tile = width // TILES
    inv_root = 1.0 / math.sqrt(width)

    rep = lax.axis_index("replica")
    ten = lax.axis_index("tensor")
    core = lax.rem(rep, 2)
    far = ten // nz
    z = lax.rem(ten, nz)
    up = (rep, far * nz + lax.rem(z + 1, nz))
    down = (rep, far * nz + lax.rem(z + nz - 1, nz))
    sibling = (rep + 1 - 2 * core, ten)
    partner = (rep + 1 - 2 * core, (1 - far) * nz + z)
    mate = (rep, (1 - far) * nz + z)
    ends = (
        (rep, far * nz + lax.rem(z + 1 - 2 * core + nz, nz)),
        (rep, far * nz + lax.rem(z - 1 + 2 * core + nz, nz)),
    )
    swapped = core + far == 1
    near = rep // (2 * ny)
    y = lax.rem(rep // 2, ny)
    across = (lax.rem(rep + 2 * ny, 4 * ny), ten)
    along = [((near * ny + lax.rem(y + d, ny)) * 2 + core, ten) for d in range(1, ny)]
    frag_rows = a_ref.shape[0]
    half_rows = frag_rows // 2
    quarter_rows = frag_rows // 4
    piece_rows = quarter_rows // ny
    half_first = core * half_rows
    quarter_first = half_first + near * quarter_rows
    piece_first = quarter_first + y * piece_rows
    col_first = pl.multiple_of((core * nz + z) * columns, columns)
    col_home = pl.multiple_of(ten * columns, columns)
    mine = core * rows
    other = (1 - core) * rows

    barrier = pltpu.get_barrier_semaphore()
    for peer in (up, down, sibling, mate, across, *along):
        pl.semaphore_signal(barrier, inc=1, device_id=peer, device_id_type=MESH)

    @pl.when(swapped)
    def _():
        pl.semaphore_signal(barrier, inc=1, device_id=partner, device_id_type=MESH)
        pl.semaphore_wait(barrier, 5 + ny)

    @pl.when(jnp.logical_not(swapped))
    def _():
        pl.semaphore_wait(barrier, 4 + ny)

    def remote(src, dst, send, recv, peer):
        return pltpu.make_async_remote_copy(
            src_ref=src, dst_ref=dst, send_sem=send, recv_sem=recv, device_id=peer, device_id_type=MESH
        )

    def x_over(j):
        return remote(
            x_ref.at[pl.ds(starts[j], sizes[j])], xb.at[0, pl.ds(other + starts[j], sizes[j])],
            own_send.at[j], got.at[0, 0, j], partner,
        )

    def w_over(k):
        return remote(
            w_ref.at[pl.ds(k * piece, piece)], wv.at[pl.ds(k * piece, piece)],
            w_send.at[k], w_recv.at[k], partner,
        )

    def x_here(j):
        return pltpu.make_async_copy(
            x_ref.at[pl.ds(starts[j], sizes[j])], xb.at[0, pl.ds(mine + starts[j], sizes[j])], got.at[0, 0, j]
        )

    def w_here(k):
        return pltpu.make_async_copy(
            w_ref.at[pl.ds(k * piece, piece)], wv.at[pl.ds(k * piece, piece)], w_recv.at[k]
        )

    late_src = x_ref.at[pl.ds(rows, LATE_ROWS)]

    def late_at(lane, step, way):
        offset = (nz - step) % nz if way == 0 else step
        return xq.at[pl.ds((lane * nz + offset) * LATE_ROWS, LATE_ROWS)]

    late_here = pltpu.make_async_copy(late_src, late_at(0, 0, 0), q_own)
    late_mate = remote(late_src, late_at(1, 0, 0), mate_send, mate_recv, mate)

    @pl.when(swapped)
    def _():
        for j in range(CHUNKS):
            x_over(j).start()

    late_here.start()
    late_mate.start()

    @pl.when(swapped)
    def _():
        for k in range(W_PIECES):
            w_over(k).start()

    @pl.when(jnp.logical_not(swapped))
    def _():
        for j in range(CHUNKS):
            x_here(j).start()
        for k in range(W_PIECES):
            w_here(k).start()

    loads = [
        pltpu.make_async_copy(src, dst, load_sem.at[k])
        for k, (src, dst) in enumerate(((w_ref, home), (a_ref, anchor), (m_ref, momentum)))
    ]
    for copy in loads:
        copy.start()

    def arrived(s, lane, j):
        place = (mine if lane == 0 else other) + starts[j]
        ref = xb.at[s, pl.ds(place, sizes[j])]
        pltpu.make_async_copy(ref, ref, got.at[s, lane, j]).wait()

    def ring(s, j):
        place = pl.ds(mine + starts[j], sizes[j])
        end = ends[0 if j in (0, CHUNKS - 1) else 1]
        return remote(xb.at[s, place], xb.at[s + 1, place], ring_send.at[s, j], got.at[s + 1, 0, j], end)

    def share(s, j):
        place = pl.ds(mine + starts[j], sizes[j])
        return remote(xb.at[s, place], xb.at[s, place], sib_send.at[s, j], got.at[s, 1, j], sibling)

    def pass_on(s, j, onward):
        arrived(s, 0, j)
        if onward:
            ring(s, j).start()
        share(s, j).start()

    def forward(s):
        for j in range(CHUNKS):
            arrived(s, 1, j)
        outputs = jnp.dot(xb[s], wv[...], preferred_element_type=jnp.float32) * inv_root
        target = xb[s, :, pl.ds(col_first, columns)].astype(jnp.float32)
        resid[...] = (outputs - target).astype(jnp.bfloat16)

    def grad_tile(s, t):
        return lax.dot_general(
            xb[s, :, pl.ds(t * tile, tile)], resid[...], (((0,), (0,)), ((), ())),
            preferred_element_type=jnp.float32,
        )

    def backward(s):
        @pl.loop(0, TILES)
        def _(t):
            t = pl.multiple_of(t * tile, tile)
            acc[pl.ds(t, tile), :] += lax.dot_general(
                xb[s, :, pl.ds(t, tile)], resid[...], (((0,), (0,)), ((), ())),
                preferred_element_type=jnp.float32,
            )

    over_core = remote(
        frag_out.at[pl.ds((1 - core) * half_rows, half_rows)], frag_in, a_send, a_recv, sibling
    )
    over_x = remote(
        part.at[pl.ds((1 - near) * quarter_rows, quarter_rows)], from_x, b_send, b_recv, across
    )
    over_y = [
        remote(
            part.at[pl.ds(near * quarter_rows + lax.rem(y + d, ny) * piece_rows, piece_rows)],
            from_y.at[d - 1], c_send.at[d - 1], c_recv.at[d - 1], along[d - 1],
        )
        for d in range(1, ny)
    ]
    piece_at = grad.at[pl.ds(piece_first, piece_rows)]
    quarter_at = grad.at[pl.ds(quarter_first, quarter_rows)]
    half_at = grad.at[pl.ds(half_first, half_rows)]
    back_y = [
        remote(piece_at, piece_at, d_send.at[d - 1], d_recv.at[d - 1], along[d - 1]) for d in range(1, ny)
    ]
    back_x = remote(quarter_at, quarter_at, e_send, e_recv, across)
    back_core = remote(half_at, half_at, f_send, f_recv, sibling)

    def chosen(k):
        return jnp.full((frag_rows, columns), frag_ref[0], jnp.int32) == k

    def sum_core():
        for copy in loads:
            copy.wait()
        rows_of = home[pl.ds(0, frag_rows), :].astype(jnp.float32)
        for k in range(1, width // frag_rows):
            block = home[pl.ds(k * frag_rows, frag_rows), :].astype(jnp.float32)
            rows_of = jnp.where(chosen(k), block, rows_of)
        frag_out[...] = rows_of.astype(jnp.bfloat16)
        over_core.start()

    def sum_x():
        over_core.wait()
        fixed = anchor[pl.ds(half_first, half_rows), :]
        own = frag_out[pl.ds(half_first, half_rows), :].astype(jnp.float32)
        part[...] = (fixed - own) + (fixed - frag_in[...].astype(jnp.float32))
        over_x.start()

    def sum_y():
        over_x.wait()
        part[pl.ds(near * quarter_rows, quarter_rows), :] += from_x[...]
        for copy in over_y:
            copy.start()

    def gather_y():
        for copy in over_y:
            copy.wait()
        total = part[pl.ds(near * quarter_rows + y * piece_rows, piece_rows), :]
        for d in range(1, ny):
            total += from_y[d - 1]
        grad[pl.ds(piece_first, piece_rows), :] = total / (4 * ny)
        for copy in back_y:
            copy.start()

    def gather_x():
        for copy in back_y:
            copy.wait()
        back_x.start()

    def gather_core():
        back_x.wait()
        back_core.start()

    stores = [
        pltpu.make_async_copy(src, dst, store_sem.at[k])
        for k, (src, dst) in enumerate(((momentum, mo_ref), (anchor, ao_ref)))
    ]

    def outer_step():
        back_core.wait()
        outer_grad = grad[...]
        moved = nesterov_mu * momentum[...] + outer_grad
        momentum[...] = moved
        anchor[...] = anchor[...] - outer_rate * (outer_grad + nesterov_mu * moved)
        for copy in stores:
            copy.start()

    def outer_stage(s):
        for k, stage_of in enumerate((sum_core, sum_x, sum_y, gather_y, gather_x, gather_core, outer_step)):
            pl.when(s == k)(stage_of)

    acc[...] = jnp.zeros_like(acc)
    half = nz // 2

    def early(s, carry):
        for j in range(CHUNKS):
            pass_on(s, j, True)
        outer_stage(s)
        return carry

    lax.fori_loop(0, half, early, 0)

    for k in range(W_PIECES):
        ref = wv.at[pl.ds(k * piece, piece)]
        pltpu.make_async_copy(ref, ref, w_recv.at[k]).wait()

    def late(s, carry):
        first = 2 * (s - half)
        pass_on(s, 0, True)
        forward(first)
        pass_on(s, 1, True)
        backward(first)
        pass_on(s, 2, True)
        forward(first + 1)
        pass_on(s, 3, True)
        backward(first + 1)
        outer_stage(s)
        return carry

    lax.fori_loop(half, nz - 1, late, 0)

    lanes = [(lane, way, half if lane == way else half - 1) for lane in range(2) for way in range(2)]

    def late_send(lane, step, way):
        return remote(
            late_at(lane, step - 1, way), late_at(lane, step, way),
            q_send.at[lane, way, step - 1], q_recv.at[lane, way, step - 1], (up, down)[way],
        )

    late_here.wait()
    late_mate.wait()
    for lane, way, most in lanes:
        late_send(lane, 1, way).start()

    last = nz - 1
    pass_on(last, 0, False)
    forward(last - 1)
    pass_on(last, 1, False)
    backward(last - 1)
    pass_on(last, 2, False)
    pass_on(last, 3, False)
    forward(last)

    def tile_at(t):
        return pl.ds(t * tile, tile)

    def relay_at(t):
        return relay.at[pl.ds(t // 2 * tile, tile)]

    def back_over(t):
        if t % 2 == 0:
            return remote(stage.at[tile_at(t)], back.at[tile_at(t)], out_send.at[t], back_recv.at[t], partner)
        return remote(stage.at[tile_at(t)], relay_at(t), out_send.at[t], relay_recv.at[t // 2], sibling)

    def back_relay(t):
        return remote(relay_at(t), back.at[tile_at(t)], relay_send.at[t // 2], back_recv.at[t], mate)

    @pl.when(swapped)
    def _():
        for t in range(TILES):
            stage[tile_at(t), :] = (acc[tile_at(t), :] + grad_tile(last, t)).astype(jnp.bfloat16)
            back_over(t).start()

    @pl.when(jnp.logical_not(swapped))
    def _():
        for t in range(TILES):
            acc[tile_at(t), :] += grad_tile(last, t)
            if t % 2 == 1:
                ref = relay_at(t)
                pltpu.make_async_copy(ref, ref, relay_recv.at[t // 2]).wait()
                back_relay(t).start()

    for step in range(1, half + 1):
        for lane, way, most in lanes:
            if step <= most:
                late_send(lane, step, way).wait_recv()
            if step < most:
                late_send(lane, step + 1, way).start()

    outputs = jnp.dot(xq[...], home[...], preferred_element_type=jnp.float32) * inv_root
    target = xq[:, pl.ds(col_home, columns)].astype(jnp.float32)
    resid_late[...] = (outputs - target).astype(jnp.bfloat16)

    def out_here(t):
        return pltpu.make_async_copy(fin.at[tile_at(t)], o_ref.at[tile_at(t)], fin_sem.at[t])

    for t in range(TILES):
        place = tile_at(t)

        @pl.when(swapped)
        def _():
            ref = back.at[place]
            pltpu.make_async_copy(ref, ref, back_recv.at[t]).wait()
            acc[place, :] = back[place, :].astype(jnp.float32)

        gradient = acc[place, :] + lax.dot_general(
            xq[:, place], resid_late[...], (((0,), (0,)), ((), ())), preferred_element_type=jnp.float32
        )
        scaled = gradient * (inv_root / total_rows)
        before = home[place, :].astype(jnp.float32)
        after = (before - inner_rate * scaled).astype(jnp.bfloat16).astype(jnp.float32)
        merged = anchor[...] + (after - before)
        fin[place, :] = jnp.where(chosen(t), merged, after).astype(jnp.bfloat16)
        out_here(t).start()

    @pl.when(swapped)
    def _():
        for j in range(CHUNKS):
            x_over(j).wait_send()
        for k in range(W_PIECES):
            w_over(k).wait_send()
        for t in range(TILES):
            back_over(t).wait_send()

    @pl.when(jnp.logical_not(swapped))
    def _():
        for t in range(1, TILES, 2):
            back_relay(t).wait_send()

    for lane, way, most in lanes:
        for step in range(1, most + 1):
            late_send(lane, step, way).wait_send()
    for t in range(TILES):
        out_here(t).wait()
    for copy in stores:
        copy.wait()

    def drain(s, carry):
        for j in range(CHUNKS):
            share(s, j).wait_send()
        return carry

    lax.fori_loop(0, nz, drain, 0)

    def drain_ring(s, carry):
        for j in range(CHUNKS):
            ring(s, j).wait_send()
        return carry

    lax.fori_loop(0, nz - 1, drain_ring, 0)


def window(nz, ny, fragment, tokens, weight, anchor, momentum):
    rows, width = tokens.shape
    columns = weight.shape[1]
    frag_rows = anchor.shape[0]
    total_rows = rows * 2 * nz
    flops = 4 * total_rows * width * columns
    whole = pl.BlockSpec(memory_space=pltpu.HBM)
    result = pl.BlockSpec(memory_space=pl.ANY)
    dma = pltpu.SemaphoreType.DMA
    return pl.pallas_call(
        functools.partial(step_kernel, nz, ny, total_rows),
        out_shape=(
            jax.ShapeDtypeStruct((width, columns), jnp.bfloat16),
            jax.ShapeDtypeStruct(momentum.shape, jnp.float32),
            jax.ShapeDtypeStruct(anchor.shape, jnp.float32),
        ),
        in_specs=[pl.BlockSpec(memory_space=pltpu.SMEM), whole, whole, whole, whole],
        out_specs=(result, result, result),
        scratch_shapes=[
            pltpu.VMEM((nz, 2 * (rows - LATE_ROWS), width), jnp.bfloat16),
            pltpu.VMEM((2 * nz * LATE_ROWS, width), jnp.bfloat16),
            pltpu.VMEM((width, columns), jnp.bfloat16),
            pltpu.VMEM((width, columns), jnp.bfloat16),
            pltpu.VMEM((width, columns), jnp.float32),
            pltpu.VMEM((2 * (rows - LATE_ROWS), columns), jnp.bfloat16),
            pltpu.VMEM((2 * nz * LATE_ROWS, columns), jnp.bfloat16),
            pltpu.VMEM((width, columns), jnp.bfloat16),
            pltpu.VMEM((width // 2, columns), jnp.bfloat16),
            pltpu.VMEM((width, columns), jnp.bfloat16),
            pltpu.VMEM((width, columns), jnp.bfloat16),
            pltpu.VMEM((frag_rows, columns), jnp.float32),
            pltpu.VMEM((frag_rows, columns), jnp.float32),
            pltpu.VMEM((frag_rows, columns), jnp.bfloat16),
            pltpu.VMEM((frag_rows // 2, columns), jnp.bfloat16),
            pltpu.VMEM((frag_rows // 2, columns), jnp.float32),
            pltpu.VMEM((frag_rows // 4, columns), jnp.float32),
            pltpu.VMEM((ny - 1, frag_rows // (4 * ny), columns), jnp.float32),
            pltpu.VMEM((frag_rows, columns), jnp.float32),
            dma((CHUNKS,)), dma((W_PIECES,)), dma((W_PIECES,)), dma((nz, 2, CHUNKS)), dma((nz - 1, CHUNKS)),
            dma((nz, CHUNKS)), dma((TILES,)), dma((TILES // 2,)), dma((TILES // 2,)), dma((TILES,)),
            dma, dma, dma, dma((2, 2, nz // 2)), dma((2, 2, nz // 2)), dma((TILES,)), dma((3,)), dma((2,)),
            dma, dma, dma, dma, dma((ny - 1,)), dma((ny - 1,)), dma((ny - 1,)), dma((ny - 1,)), dma, dma, dma, dma,
        ],
        cost_estimate=pl.CostEstimate(flops=flops, bytes_accessed=8 << 20, transcendentals=0),
        compiler_params=pltpu.CompilerParams(
            collective_id=0, has_side_effects=True, vmem_limit_bytes=54 << 20
        ),
    )(fragment, tokens, weight, anchor, momentum)


def local(nz, ny, params, anchor, momentum, tokens, fragment):
    params_out, momentum_out, anchor_out = window(
        nz, ny, fragment, tokens[0, 0], params[0], anchor, momentum
    )
    return (params_out[None], momentum_out, anchor_out)


def solution(mesh):
    return jax.shard_map(
        functools.partial(local, mesh.shape["tensor"] // 2, mesh.shape["replica"] // 4),
        mesh=mesh,
        in_specs=(
            P("replica", None, "tensor"),
            P(None, "tensor"),
            P(None, "tensor"),
            P("replica", None, "tensor", None),
            P(),
        ),
        out_specs=(P("replica", None, "tensor"), P(None, "tensor"), P(None, "tensor")),
        check_vma=False,
    )
```

```python
import functools
import math

import jax
import jax.numpy as jnp
from jax import lax
from jax.experimental import pallas as pl
from jax.experimental.pallas import tpu as pltpu
from jax.sharding import PartitionSpec as P

LATE_ROWS = 16
PARTS = (2, 2, 2, 1)
CHUNKS = len(PARTS)
W_PIECES = 8
TILES = 8

inner_rate = 128.0
outer_rate = 0.7
nesterov_mu = 0.9

MESH = pl.DeviceIdType.MESH


def step_kernel(
    nz, ny, total_rows, frag_ref, x_ref, w_ref, a_ref, m_ref, o_ref, mo_ref, ao_ref,
    xb, xq, wv, home, acc, resid, resid_late, stage, relay, back, fin,
    anchor, momentum, frag_out, frag_in, part, from_x, from_y, grad,
    own_send, w_send, w_recv, got, ring_send, sib_send, out_send, relay_recv, relay_send, back_recv,
    q_own, mate_send, mate_recv, q_send, q_recv, fin_sem, load_sem, store_sem,
    a_send, a_recv, b_send, b_recv, c_send, c_recv, d_send, d_recv, e_send, e_recv, f_send, f_recv,
):
    shard, width = x_ref.shape
    rows = shard - LATE_ROWS
    columns = w_ref.shape[1]
    sizes = [rows * part // 7 for part in PARTS]
    starts = [sum(sizes[:j]) for j in range(CHUNKS)]
    piece = width // W_PIECES
    tile = width // TILES
    inv_root = 1.0 / math.sqrt(width)

    rep = lax.axis_index("replica")
    ten = lax.axis_index("tensor")
    core = lax.rem(rep, 2)
    far = ten // nz
    z = lax.rem(ten, nz)
    up = (rep, far * nz + lax.rem(z + 1, nz))
    down = (rep, far * nz + lax.rem(z + nz - 1, nz))
    sibling = (rep + 1 - 2 * core, ten)
    partner = (rep + 1 - 2 * core, (1 - far) * nz + z)
    mate = (rep, (1 - far) * nz + z)
    ends = (
        (rep, far * nz + lax.rem(z + 1 - 2 * core + nz, nz)),
        (rep, far * nz + lax.rem(z - 1 + 2 * core + nz, nz)),
    )
    swapped = core + far == 1
    near = rep // (2 * ny)
    y = lax.rem(rep // 2, ny)
    across = (lax.rem(rep + 2 * ny, 4 * ny), ten)
    along = [((near * ny + lax.rem(y + d, ny)) * 2 + core, ten) for d in range(1, ny)]
    frag_rows = a_ref.shape[0]
    half_rows = frag_rows // 2
    quarter_rows = frag_rows // 4
    piece_rows = quarter_rows // ny
    half_first = core * half_rows
    quarter_first = half_first + near * quarter_rows
    piece_first = quarter_first + y * piece_rows
    col_first = pl.multiple_of((core * nz + z) * columns, columns)
    col_home = pl.multiple_of(ten * columns, columns)
    mine = core * rows
    other = (1 - core) * rows

    barrier = pltpu.get_barrier_semaphore()
    for peer in (up, down, sibling, mate, across, *along):
        pl.semaphore_signal(barrier, inc=1, device_id=peer, device_id_type=MESH)

    @pl.when(swapped)
    def _():
        pl.semaphore_signal(barrier, inc=1, device_id=partner, device_id_type=MESH)
        pl.semaphore_wait(barrier, 5 + ny)

    @pl.when(jnp.logical_not(swapped))
    def _():
        pl.semaphore_wait(barrier, 4 + ny)

    def remote(src, dst, send, recv, peer):
        return pltpu.make_async_remote_copy(
            src_ref=src, dst_ref=dst, send_sem=send, recv_sem=recv, device_id=peer, device_id_type=MESH
        )

    def x_over(j):
        return remote(
            x_ref.at[pl.ds(starts[j], sizes[j])], xb.at[0, pl.ds(other + starts[j], sizes[j])],
            own_send.at[j], got.at[0, 0, j], partner,
        )

    def w_over(k):
        return remote(
            w_ref.at[pl.ds(k * piece, piece)], wv.at[pl.ds(k * piece, piece)],
            w_send.at[k], w_recv.at[k], partner,
        )

    def x_here(j):
        return pltpu.make_async_copy(
            x_ref.at[pl.ds(starts[j], sizes[j])], xb.at[0, pl.ds(mine + starts[j], sizes[j])], got.at[0, 0, j]
        )

    def w_here(k):
        return pltpu.make_async_copy(
            w_ref.at[pl.ds(k * piece, piece)], wv.at[pl.ds(k * piece, piece)], w_recv.at[k]
        )

    late_src = x_ref.at[pl.ds(rows, LATE_ROWS)]

    def late_at(lane, step, way):
        offset = (nz - step) % nz if way == 0 else step
        return xq.at[pl.ds((lane * nz + offset) * LATE_ROWS, LATE_ROWS)]

    late_here = pltpu.make_async_copy(late_src, late_at(0, 0, 0), q_own)
    late_mate = remote(late_src, late_at(1, 0, 0), mate_send, mate_recv, mate)

    @pl.when(swapped)
    def _():
        for j in range(CHUNKS):
            x_over(j).start()

    late_here.start()
    late_mate.start()

    @pl.when(swapped)
    def _():
        for k in range(W_PIECES):
            w_over(k).start()

    @pl.when(jnp.logical_not(swapped))
    def _():
        for j in range(CHUNKS):
            x_here(j).start()
        for k in range(W_PIECES):
            w_here(k).start()

    loads = [
        pltpu.make_async_copy(src, dst, load_sem.at[k])
        for k, (src, dst) in enumerate(((w_ref, home), (a_ref, anchor), (m_ref, momentum)))
    ]
    for copy in loads:
        copy.start()

    def arrived(s, lane, j):
        place = (mine if lane == 0 else other) + starts[j]
        ref = xb.at[s, pl.ds(place, sizes[j])]
        pltpu.make_async_copy(ref, ref, got.at[s, lane, j]).wait()

    def ring(s, j):
        place = pl.ds(mine + starts[j], sizes[j])
        end = ends[0 if j in (0, CHUNKS - 1) else 1]
        return remote(xb.at[s, place], xb.at[s + 1, place], ring_send.at[s, j], got.at[s + 1, 0, j], end)

    def share(s, j):
        place = pl.ds(mine + starts[j], sizes[j])
        return remote(xb.at[s, place], xb.at[s, place], sib_send.at[s, j], got.at[s, 1, j], sibling)

    def pass_on(s, j, onward):
        arrived(s, 0, j)
        if onward:
            ring(s, j).start()
        share(s, j).start()

    def forward(s):
        for j in range(CHUNKS):
            arrived(s, 1, j)
        outputs = jnp.dot(xb[s], wv[...], preferred_element_type=jnp.float32) * inv_root
        target = xb[s, :, pl.ds(col_first, columns)].astype(jnp.float32)
        resid[...] = (outputs - target).astype(jnp.bfloat16)

    def grad_tile(s, t):
        return lax.dot_general(
            xb[s, :, pl.ds(t * tile, tile)], resid[...], (((0,), (0,)), ((), ())),
            preferred_element_type=jnp.float32,
        )

    def backward(s):
        @pl.loop(0, TILES)
        def _(t):
            t = pl.multiple_of(t * tile, tile)
            acc[pl.ds(t, tile), :] += lax.dot_general(
                xb[s, :, pl.ds(t, tile)], resid[...], (((0,), (0,)), ((), ())),
                preferred_element_type=jnp.float32,
            )

    over_core = remote(
        frag_out.at[pl.ds((1 - core) * half_rows, half_rows)], frag_in, a_send, a_recv, sibling
    )
    over_x = remote(
        part.at[pl.ds((1 - near) * quarter_rows, quarter_rows)], from_x, b_send, b_recv, across
    )
    over_y = [
        remote(
            part.at[pl.ds(near * quarter_rows + lax.rem(y + d, ny) * piece_rows, piece_rows)],
            from_y.at[d - 1], c_send.at[d - 1], c_recv.at[d - 1], along[d - 1],
        )
        for d in range(1, ny)
    ]
    piece_at = grad.at[pl.ds(piece_first, piece_rows)]
    quarter_at = grad.at[pl.ds(quarter_first, quarter_rows)]
    half_at = grad.at[pl.ds(half_first, half_rows)]
    back_y = [
        remote(piece_at, piece_at, d_send.at[d - 1], d_recv.at[d - 1], along[d - 1]) for d in range(1, ny)
    ]
    back_x = remote(quarter_at, quarter_at, e_send, e_recv, across)
    back_core = remote(half_at, half_at, f_send, f_recv, sibling)

    def chosen(k):
        return jnp.full((frag_rows, columns), frag_ref[0], jnp.int32) == k

    def sum_core():
        for copy in loads:
            copy.wait()
        rows_of = home[pl.ds(0, frag_rows), :].astype(jnp.float32)
        for k in range(1, width // frag_rows):
            block = home[pl.ds(k * frag_rows, frag_rows), :].astype(jnp.float32)
            rows_of = jnp.where(chosen(k), block, rows_of)
        frag_out[...] = rows_of.astype(jnp.bfloat16)
        over_core.start()

    def sum_x():
        over_core.wait()
        fixed = anchor[pl.ds(half_first, half_rows), :]
        own = frag_out[pl.ds(half_first, half_rows), :].astype(jnp.float32)
        part[...] = (fixed - own) + (fixed - frag_in[...].astype(jnp.float32))
        over_x.start()

    def sum_y():
        over_x.wait()
        part[pl.ds(near * quarter_rows, quarter_rows), :] += from_x[...]
        for copy in over_y:
            copy.start()

    def gather_y():
        for copy in over_y:
            copy.wait()
        total = part[pl.ds(near * quarter_rows + y * piece_rows, piece_rows), :]
        for d in range(1, ny):
            total += from_y[d - 1]
        grad[pl.ds(piece_first, piece_rows), :] = total / (4 * ny)
        for copy in back_y:
            copy.start()

    def gather_x():
        for copy in back_y:
            copy.wait()
        back_x.start()

    def gather_core():
        back_x.wait()
        back_core.start()

    stores = [
        pltpu.make_async_copy(src, dst, store_sem.at[k])
        for k, (src, dst) in enumerate(((momentum, mo_ref), (anchor, ao_ref)))
    ]

    def outer_step():
        back_core.wait()
        outer_grad = grad[...]
        moved = nesterov_mu * momentum[...] + outer_grad
        momentum[...] = moved
        anchor[...] = anchor[...] - outer_rate * (outer_grad + nesterov_mu * moved)
        for copy in stores:
            copy.start()

    def outer_stage(s):
        for k, stage_of in enumerate((sum_core, sum_x, sum_y, gather_y, gather_x, gather_core, outer_step)):
            pl.when(s == k)(stage_of)

    acc[...] = jnp.zeros_like(acc)
    half = nz // 2

    def early(s, carry):
        for j in range(CHUNKS):
            pass_on(s, j, True)
        outer_stage(s)
        return carry

    lax.fori_loop(0, half, early, 0)

    for k in range(W_PIECES):
        ref = wv.at[pl.ds(k * piece, piece)]
        pltpu.make_async_copy(ref, ref, w_recv.at[k]).wait()

    def late(s, carry):
        first = 2 * (s - half)
        pass_on(s, 0, True)
        forward(first)
        pass_on(s, 1, True)
        backward(first)
        pass_on(s, 2, True)
        forward(first + 1)
        pass_on(s, 3, True)
        backward(first + 1)
        outer_stage(s)
        return carry

    lax.fori_loop(half, nz - 1, late, 0)

    lanes = [(lane, way, half if lane == way else half - 1) for lane in range(2) for way in range(2)]

    def late_send(lane, step, way):
        return remote(
            late_at(lane, step - 1, way), late_at(lane, step, way),
            q_send.at[lane, way, step - 1], q_recv.at[lane, way, step - 1], (up, down)[way],
        )

    late_here.wait()
    late_mate.wait()
    for lane, way, most in lanes:
        late_send(lane, 1, way).start()

    last = nz - 1
    pass_on(last, 0, False)
    forward(last - 1)
    pass_on(last, 1, False)
    backward(last - 1)
    pass_on(last, 2, False)
    pass_on(last, 3, False)
    forward(last)

    def tile_at(t):
        return pl.ds(t * tile, tile)

    def relay_at(t):
        return relay.at[pl.ds(t // 2 * tile, tile)]

    def back_over(t):
        if t % 2 == 0:
            return remote(stage.at[tile_at(t)], back.at[tile_at(t)], out_send.at[t], back_recv.at[t], partner)
        return remote(stage.at[tile_at(t)], relay_at(t), out_send.at[t], relay_recv.at[t // 2], sibling)

    def back_relay(t):
        return remote(relay_at(t), back.at[tile_at(t)], relay_send.at[t // 2], back_recv.at[t], mate)

    @pl.when(swapped)
    def _():
        for t in range(TILES):
            stage[tile_at(t), :] = (acc[tile_at(t), :] + grad_tile(last, t)).astype(jnp.bfloat16)
            back_over(t).start()

    @pl.when(jnp.logical_not(swapped))
    def _():
        for t in range(TILES):
            acc[tile_at(t), :] += grad_tile(last, t)
            if t % 2 == 1:
                ref = relay_at(t)
                pltpu.make_async_copy(ref, ref, relay_recv.at[t // 2]).wait()
                back_relay(t).start()

    for step in range(1, half + 1):
        for lane, way, most in lanes:
            if step <= most:
                late_send(lane, step, way).wait_recv()
            if step < most:
                late_send(lane, step + 1, way).start()

    outputs = jnp.dot(xq[...], home[...], preferred_element_type=jnp.float32) * inv_root
    target = xq[:, pl.ds(col_home, columns)].astype(jnp.float32)
    resid_late[...] = (outputs - target).astype(jnp.bfloat16)

    def out_here(t):
        return pltpu.make_async_copy(fin.at[tile_at(t)], o_ref.at[tile_at(t)], fin_sem.at[t])

    for t in range(TILES):
        place = tile_at(t)

        @pl.when(swapped)
        def _():
            ref = back.at[place]
            pltpu.make_async_copy(ref, ref, back_recv.at[t]).wait()
            acc[place, :] = back[place, :].astype(jnp.float32)

        gradient = acc[place, :] + lax.dot_general(
            xq[:, place], resid_late[...], (((0,), (0,)), ((), ())), preferred_element_type=jnp.float32
        )
        scaled = gradient * (inv_root / total_rows)
        before = home[place, :].astype(jnp.float32)
        after = (before - inner_rate * scaled).astype(jnp.bfloat16).astype(jnp.float32)
        merged = anchor[...] + (after - before)
        fin[place, :] = jnp.where(chosen(t), merged, after).astype(jnp.bfloat16)
        out_here(t).start()

    @pl.when(swapped)
    def _():
        for j in range(CHUNKS):
            x_over(j).wait_send()
        for k in range(W_PIECES):
            w_over(k).wait_send()
        for t in range(TILES):
            back_over(t).wait_send()

    @pl.when(jnp.logical_not(swapped))
    def _():
        for t in range(1, TILES, 2):
            back_relay(t).wait_send()

    for lane, way, most in lanes:
        for step in range(1, most + 1):
            late_send(lane, step, way).wait_send()
    for t in range(TILES):
        out_here(t).wait()
    for copy in stores:
        copy.wait()

    def drain(s, carry):
        for j in range(CHUNKS):
            share(s, j).wait_send()
        return carry

    lax.fori_loop(0, nz, drain, 0)

    def drain_ring(s, carry):
        for j in range(CHUNKS):
            ring(s, j).wait_send()
        return carry

    lax.fori_loop(0, nz - 1, drain_ring, 0)


def window(nz, ny, fragment, tokens, weight, anchor, momentum):
    rows, width = tokens.shape
    columns = weight.shape[1]
    frag_rows = anchor.shape[0]
    total_rows = rows * 2 * nz
    flops = 4 * total_rows * width * columns
    whole = pl.BlockSpec(memory_space=pltpu.HBM)
    result = pl.BlockSpec(memory_space=pl.ANY)
    dma = pltpu.SemaphoreType.DMA
    return pl.pallas_call(
        functools.partial(step_kernel, nz, ny, total_rows),
        out_shape=(
            pltpu.VMEM((width, columns), jnp.bfloat16),
            pltpu.VMEM(momentum.shape, jnp.float32),
            pltpu.VMEM(anchor.shape, jnp.float32),
        ),
        in_specs=[pl.BlockSpec(memory_space=pltpu.SMEM), whole, whole, whole, whole],
        out_specs=(result, result, result),
        scratch_shapes=[
            pltpu.VMEM((nz, 2 * (rows - LATE_ROWS), width), jnp.bfloat16),
            pltpu.VMEM((2 * nz * LATE_ROWS, width), jnp.bfloat16),
            pltpu.VMEM((width, columns), jnp.bfloat16),
            pltpu.VMEM((width, columns), jnp.bfloat16),
            pltpu.VMEM((width, columns), jnp.float32),
            pltpu.VMEM((2 * (rows - LATE_ROWS), columns), jnp.bfloat16),
            pltpu.VMEM((2 * nz * LATE_ROWS, columns), jnp.bfloat16),
            pltpu.VMEM((width, columns), jnp.bfloat16),
            pltpu.VMEM((width // 2, columns), jnp.bfloat16),
            pltpu.VMEM((width, columns), jnp.bfloat16),
            pltpu.VMEM((width, columns), jnp.bfloat16),
            pltpu.VMEM((frag_rows, columns), jnp.float32),
            pltpu.VMEM((frag_rows, columns), jnp.float32),
            pltpu.VMEM((frag_rows, columns), jnp.bfloat16),
            pltpu.VMEM((frag_rows // 2, columns), jnp.bfloat16),
            pltpu.VMEM((frag_rows // 2, columns), jnp.float32),
            pltpu.VMEM((frag_rows // 4, columns), jnp.float32),
            pltpu.VMEM((ny - 1, frag_rows // (4 * ny), columns), jnp.float32),
            pltpu.VMEM((frag_rows, columns), jnp.float32),
            dma((CHUNKS,)), dma((W_PIECES,)), dma((W_PIECES,)), dma((nz, 2, CHUNKS)), dma((nz - 1, CHUNKS)),
            dma((nz, CHUNKS)), dma((TILES,)), dma((TILES // 2,)), dma((TILES // 2,)), dma((TILES,)),
            dma, dma, dma, dma((2, 2, nz // 2)), dma((2, 2, nz // 2)), dma((TILES,)), dma((3,)), dma((2,)),
            dma, dma, dma, dma, dma((ny - 1,)), dma((ny - 1,)), dma((ny - 1,)), dma((ny - 1,)), dma, dma, dma, dma,
        ],
        cost_estimate=pl.CostEstimate(flops=flops, bytes_accessed=8 << 20, transcendentals=0),
        compiler_params=pltpu.CompilerParams(
            collective_id=0, has_side_effects=True, vmem_limit_bytes=59 << 20
        ),
    )(fragment, tokens, weight, anchor, momentum)


def local(nz, ny, params, anchor, momentum, tokens, fragment):
    params_out, momentum_out, anchor_out = window(
        nz, ny, fragment, tokens[0, 0], params[0], anchor, momentum
    )
    return (params_out[None], momentum_out, anchor_out)


def solution(mesh):
    return jax.shard_map(
        functools.partial(local, mesh.shape["tensor"] // 2, mesh.shape["replica"] // 4),
        mesh=mesh,
        in_specs=(
            P("replica", None, "tensor"),
            P(None, "tensor"),
            P(None, "tensor"),
            P("replica", None, "tensor", None),
            P(),
        ),
        out_specs=(P("replica", None, "tensor"), P(None, "tensor"), P(None, "tensor")),
        check_vma=False,
    )
```

```python
import functools
import math

import jax
import jax.numpy as jnp
from jax import lax
from jax.experimental import pallas as pl
from jax.experimental.pallas import tpu as pltpu
from jax.sharding import PartitionSpec as P

PARTS = (3, 1, 3, 1)
CHUNKS = len(PARTS)
W_PIECES = 8
TILES = 8

inner_rate = 128.0
outer_rate = 0.7
nesterov_mu = 0.9

MESH = pl.DeviceIdType.MESH


def step_kernel(
    nz, ny, total_rows, frag_ref, x_ref, w_ref, a_ref, m_ref, o_ref, mo_ref, ao_ref,
    xb, xq, xm, wv, home, acc, resid, resid_late, stage, relay, back, fin,
    anchor, momentum, frag_out, frag_in, part, from_x, from_y, grad,
    own_send, w_send, w_recv, got, ring_send, sib_send, out_send, relay_recv, relay_send, back_recv,
    mate_send, mate_recv, q_send, q_recv, fin_sem, load_sem, store_sem,
    a_send, a_recv, b_send, b_recv, c_send, c_recv, d_send, d_recv, e_send, e_recv, f_send, f_recv,
):
    rows, width = x_ref.shape
    side = rows // 2
    last = nz - 2
    columns = w_ref.shape[1]
    sizes = [rows * part // 8 for part in PARTS]
    starts = [sum(sizes[:j]) for j in range(CHUNKS)]
    piece = width // W_PIECES
    tile = width // TILES
    inv_root = 1.0 / math.sqrt(width)

    rep = lax.axis_index("replica")
    ten = lax.axis_index("tensor")
    core = lax.rem(rep, 2)
    far = ten // nz
    z = lax.rem(ten, nz)
    up = (rep, far * nz + lax.rem(z + 1, nz))
    down = (rep, far * nz + lax.rem(z + nz - 1, nz))
    sibling = (rep + 1 - 2 * core, ten)
    partner = (rep + 1 - 2 * core, (1 - far) * nz + z)
    mate = (rep, (1 - far) * nz + z)
    swapped = core + far == 1
    near = rep // (2 * ny)
    y = lax.rem(rep // 2, ny)
    across = (lax.rem(rep + 2 * ny, 4 * ny), ten)
    along = [((near * ny + lax.rem(y + d, ny)) * 2 + core, ten) for d in range(1, ny)]
    frag_rows = a_ref.shape[0]
    half_rows = frag_rows // 2
    quarter_rows = frag_rows // 4
    piece_rows = quarter_rows // ny
    half_first = core * half_rows
    quarter_first = half_first + near * quarter_rows
    piece_first = quarter_first + y * piece_rows
    col_first = pl.multiple_of((core * nz + z) * columns, columns)
    col_home = pl.multiple_of(ten * columns, columns)
    mine = core * rows
    other = (1 - core) * rows

    barrier = pltpu.get_barrier_semaphore()
    for peer in (up, down, sibling, mate, across, *along):
        pl.semaphore_signal(barrier, inc=1, device_id=peer, device_id_type=MESH)

    @pl.when(swapped)
    def _():
        pl.semaphore_signal(barrier, inc=1, device_id=partner, device_id_type=MESH)
        pl.semaphore_wait(barrier, 5 + ny)

    @pl.when(jnp.logical_not(swapped))
    def _():
        pl.semaphore_wait(barrier, 4 + ny)

    def remote(src, dst, send, recv, peer):
        return pltpu.make_async_remote_copy(
            src_ref=src, dst_ref=dst, send_sem=send, recv_sem=recv, device_id=peer, device_id_type=MESH
        )

    def x_over(j):
        return remote(
            x_ref.at[pl.ds(starts[j], sizes[j])], xb.at[0, pl.ds(other + starts[j], sizes[j])],
            own_send.at[j], got.at[0, 0, j], partner,
        )

    def w_over(k):
        return remote(
            w_ref.at[pl.ds(k * piece, piece)], wv.at[pl.ds(k * piece, piece)],
            w_send.at[k], w_recv.at[k], partner,
        )

    def x_here(j):
        return pltpu.make_async_copy(
            x_ref.at[pl.ds(starts[j], sizes[j])], xb.at[0, pl.ds(mine + starts[j], sizes[j])], got.at[0, 0, j]
        )

    def w_here(k):
        return pltpu.make_async_copy(
            w_ref.at[pl.ds(k * piece, piece)], wv.at[pl.ds(k * piece, piece)], w_recv.at[k]
        )

    late_mate = remote(x_ref, xm, mate_send, mate_recv, mate)

    @pl.when(swapped)
    def _():
        for j in range(CHUNKS):
            x_over(j).start()

    @pl.when(swapped)
    def _():
        for k in range(W_PIECES):
            w_over(k).start()

    @pl.when(jnp.logical_not(swapped))
    def _():
        for j in range(CHUNKS):
            x_here(j).start()
        for k in range(W_PIECES):
            w_here(k).start()

    loads = [
        pltpu.make_async_copy(src, dst, load_sem.at[k])
        for k, (src, dst) in enumerate(((w_ref, home), (a_ref, anchor), (m_ref, momentum)))
    ]
    for copy in loads:
        copy.start()

    def arrived(s, lane, j):
        place = (mine if lane == 0 else other) + starts[j]
        ref = xb.at[s, pl.ds(place, sizes[j])]
        pltpu.make_async_copy(ref, ref, got.at[s, lane, j]).wait()

    def ring(s, j):
        place = pl.ds(mine + starts[j], sizes[j])
        end = up if starts[j] < side else down
        return remote(xb.at[s, place], xb.at[s + 1, place], ring_send.at[s, j], got.at[s + 1, 0, j], end)

    def share(s, j):
        place = pl.ds(mine + starts[j], sizes[j])
        return remote(xb.at[s, place], xb.at[s, place], sib_send.at[s, j], got.at[s, 1, j], sibling)

    def pass_on(s, j, onward):
        arrived(s, 0, j)
        if onward:
            ring(s, j).start()
        share(s, j).start()

    def forward(s):
        for j in range(CHUNKS):
            arrived(s, 1, j)
        outputs = jnp.dot(xb[s], wv[...], preferred_element_type=jnp.float32) * inv_root
        target = xb[s, :, pl.ds(col_first, columns)].astype(jnp.float32)
        resid[...] = (outputs - target).astype(jnp.bfloat16)

    def grad_tile(s, t):
        return lax.dot_general(
            xb[s, :, pl.ds(t * tile, tile)], resid[...], (((0,), (0,)), ((), ())),
            preferred_element_type=jnp.float32,
        )

    def backward(s):
        @pl.loop(0, TILES)
        def _(t):
            t = pl.multiple_of(t * tile, tile)
            acc[pl.ds(t, tile), :] += lax.dot_general(
                xb[s, :, pl.ds(t, tile)], resid[...], (((0,), (0,)), ((), ())),
                preferred_element_type=jnp.float32,
            )

    over_core = remote(
        frag_out.at[pl.ds((1 - core) * half_rows, half_rows)], frag_in, a_send, a_recv, sibling
    )
    over_x = remote(
        part.at[pl.ds((1 - near) * quarter_rows, quarter_rows)], from_x, b_send, b_recv, across
    )
    over_y = [
        remote(
            part.at[pl.ds(near * quarter_rows + lax.rem(y + d, ny) * piece_rows, piece_rows)],
            from_y.at[d - 1], c_send.at[d - 1], c_recv.at[d - 1], along[d - 1],
        )
        for d in range(1, ny)
    ]
    piece_at = grad.at[pl.ds(piece_first, piece_rows)]
    quarter_at = grad.at[pl.ds(quarter_first, quarter_rows)]
    half_at = grad.at[pl.ds(half_first, half_rows)]
    back_y = [
        remote(piece_at, piece_at, d_send.at[d - 1], d_recv.at[d - 1], along[d - 1]) for d in range(1, ny)
    ]
    back_x = remote(quarter_at, quarter_at, e_send, e_recv, across)
    back_core = remote(half_at, half_at, f_send, f_recv, sibling)

    def chosen(k):
        return jnp.full((frag_rows, columns), frag_ref[0], jnp.int32) == k

    def sum_core():
        for copy in loads:
            copy.wait()
        rows_of = home[pl.ds(0, frag_rows), :].astype(jnp.float32)
        for k in range(1, width // frag_rows):
            block = home[pl.ds(k * frag_rows, frag_rows), :].astype(jnp.float32)
            rows_of = jnp.where(chosen(k), block, rows_of)
        frag_out[...] = rows_of.astype(jnp.bfloat16)
        over_core.start()

    def sum_x():
        over_core.wait()
        fixed = anchor[pl.ds(half_first, half_rows), :]
        own = frag_out[pl.ds(half_first, half_rows), :].astype(jnp.float32)
        part[...] = (fixed - own) + (fixed - frag_in[...].astype(jnp.float32))
        over_x.start()

    def sum_y():
        over_x.wait()
        part[pl.ds(near * quarter_rows, quarter_rows), :] += from_x[...]
        for copy in over_y:
            copy.start()

    def gather_y():
        for copy in over_y:
            copy.wait()
        total = part[pl.ds(near * quarter_rows + y * piece_rows, piece_rows), :]
        for d in range(1, ny):
            total += from_y[d - 1]
        grad[pl.ds(piece_first, piece_rows), :] = total / (4 * ny)
        for copy in back_y:
            copy.start()

    def gather_x():
        for copy in back_y:
            copy.wait()
        back_x.start()

    def gather_core():
        back_x.wait()
        back_core.start()

    stores = [
        pltpu.make_async_copy(src, dst, store_sem.at[k])
        for k, (src, dst) in enumerate(((momentum, mo_ref), (anchor, ao_ref)))
    ]

    def outer_step():
        back_core.wait()
        outer_grad = grad[...]
        moved = nesterov_mu * momentum[...] + outer_grad
        momentum[...] = moved
        anchor[...] = anchor[...] - outer_rate * (outer_grad + nesterov_mu * moved)
        for copy in stores:
            copy.start()

    def outer_stage(s):
        for k, stage_of in enumerate((sum_core, sum_x, sum_y, gather_y, gather_x, gather_core)):
            pl.when(s == k)(stage_of)

    acc[...] = jnp.zeros_like(acc)
    half = nz // 2

    def early(s, carry):
        for j in range(CHUNKS):
            pass_on(s, j, True)
        outer_stage(s)
        pl.when(s == 2)(late_mate.start)
        return carry

    lax.fori_loop(0, half, early, 0)

    for k in range(W_PIECES):
        ref = wv.at[pl.ds(k * piece, piece)]
        pltpu.make_async_copy(ref, ref, w_recv.at[k]).wait()

    def late(s, carry):
        first = 2 * (s - half)
        pass_on(s, 0, True)
        forward(first)
        pass_on(s, 1, True)
        backward(first)
        pass_on(s, 2, True)
        forward(first + 1)
        pass_on(s, 3, True)
        backward(first + 1)
        outer_stage(s)
        return carry

    lax.fori_loop(half, last, late, 0)

    def late_send(lane, way):
        source = (x_ref, xm)[lane].at[pl.ds(way * side, side)]
        slot = xq.at[pl.ds((lane * 2 + way) * side, side)]
        return remote(source, slot, q_send.at[lane, way], q_recv.at[lane, way], (down, up)[way])

    late = [late_send(lane, way) for lane in range(2) for way in range(2)]

    pass_on(last, 0, False)
    forward(last - 2)
    backward(last - 2)
    pass_on(last, 1, False)
    forward(last - 1)
    backward(last - 1)
    late_mate.wait()
    pass_on(last, 2, False)
    pass_on(last, 3, False)
    for copy in late:
        copy.start()
    forward(last)

    def tile_at(t):
        return pl.ds(t * tile, tile)

    def relay_at(t):
        return relay.at[pl.ds(t // 2 * tile, tile)]

    def back_over(t):
        if t % 2 == 0:
            return remote(stage.at[tile_at(t)], back.at[tile_at(t)], out_send.at[t], back_recv.at[t], partner)
        return remote(stage.at[tile_at(t)], relay_at(t), out_send.at[t], relay_recv.at[t // 2], sibling)

    def back_relay(t):
        return remote(relay_at(t), back.at[tile_at(t)], relay_send.at[t // 2], back_recv.at[t], mate)

    @pl.when(swapped)
    def _():
        for t in range(TILES):
            stage[tile_at(t), :] = (acc[tile_at(t), :] + grad_tile(last, t)).astype(jnp.bfloat16)
            back_over(t).start()

    @pl.when(jnp.logical_not(swapped))
    def _():
        for t in range(TILES):
            acc[tile_at(t), :] += grad_tile(last, t)
            if t % 2 == 1:
                ref = relay_at(t)
                pltpu.make_async_copy(ref, ref, relay_recv.at[t // 2]).wait()
                back_relay(t).start()

    outer_step()
    for copy in late:
        copy.wait_recv()

    outputs = jnp.dot(xq[...], home[...], preferred_element_type=jnp.float32) * inv_root
    target = xq[:, pl.ds(col_home, columns)].astype(jnp.float32)
    resid_late[...] = (outputs - target).astype(jnp.bfloat16)

    def out_here(t):
        return pltpu.make_async_copy(fin.at[tile_at(t)], o_ref.at[tile_at(t)], fin_sem.at[t])

    for t in range(TILES):
        place = tile_at(t)

        @pl.when(swapped)
        def _():
            ref = back.at[place]
            pltpu.make_async_copy(ref, ref, back_recv.at[t]).wait()
            acc[place, :] = back[place, :].astype(jnp.float32)

        gradient = acc[place, :] + lax.dot_general(
            xq[:, place], resid_late[...], (((0,), (0,)), ((), ())), preferred_element_type=jnp.float32
        )
        scaled = gradient * (inv_root / total_rows)
        before = home[place, :].astype(jnp.float32)
        after = (before - inner_rate * scaled).astype(jnp.bfloat16).astype(jnp.float32)
        merged = anchor[...] + (after - before)
        fin[place, :] = jnp.where(chosen(t), merged, after).astype(jnp.bfloat16)
        out_here(t).start()

    @pl.when(swapped)
    def _():
        for j in range(CHUNKS):
            x_over(j).wait_send()
        for k in range(W_PIECES):
            w_over(k).wait_send()
        for t in range(TILES):
            back_over(t).wait_send()

    @pl.when(jnp.logical_not(swapped))
    def _():
        for t in range(1, TILES, 2):
            back_relay(t).wait_send()

    for copy in late:
        copy.wait_send()
    for t in range(TILES):
        out_here(t).wait()
    for copy in stores:
        copy.wait()

    def drain(s, carry):
        for j in range(CHUNKS):
            share(s, j).wait_send()
        return carry

    lax.fori_loop(0, last + 1, drain, 0)

    def drain_ring(s, carry):
        for j in range(CHUNKS):
            ring(s, j).wait_send()
        return carry

    lax.fori_loop(0, last, drain_ring, 0)


def window(nz, ny, fragment, tokens, weight, anchor, momentum):
    rows, width = tokens.shape
    columns = weight.shape[1]
    frag_rows = anchor.shape[0]
    total_rows = rows * 2 * nz
    flops = 4 * total_rows * width * columns
    whole = pl.BlockSpec(memory_space=pltpu.HBM)
    result = pl.BlockSpec(memory_space=pl.ANY)
    dma = pltpu.SemaphoreType.DMA
    return pl.pallas_call(
        functools.partial(step_kernel, nz, ny, total_rows),
        out_shape=(
            pltpu.VMEM((width, columns), jnp.bfloat16),
            pltpu.VMEM(momentum.shape, jnp.float32),
            pltpu.VMEM(anchor.shape, jnp.float32),
        ),
        in_specs=[pl.BlockSpec(memory_space=pltpu.SMEM), whole, whole, whole, whole],
        out_specs=(result, result, result),
        scratch_shapes=[
            pltpu.VMEM((nz - 1, 2 * rows, width), jnp.bfloat16),
            pltpu.VMEM((2 * rows, width), jnp.bfloat16),
            pltpu.VMEM((rows, width), jnp.bfloat16),
            pltpu.VMEM((width, columns), jnp.bfloat16),
            pltpu.VMEM((width, columns), jnp.bfloat16),
            pltpu.VMEM((width, columns), jnp.float32),
            pltpu.VMEM((2 * rows, columns), jnp.bfloat16),
            pltpu.VMEM((2 * rows, columns), jnp.bfloat16),
            pltpu.VMEM((width, columns), jnp.bfloat16),
            pltpu.VMEM((width // 2, columns), jnp.bfloat16),
            pltpu.VMEM((width, columns), jnp.bfloat16),
            pltpu.VMEM((width, columns), jnp.bfloat16),
            pltpu.VMEM((frag_rows, columns), jnp.float32),
            pltpu.VMEM((frag_rows, columns), jnp.float32),
            pltpu.VMEM((frag_rows, columns), jnp.bfloat16),
            pltpu.VMEM((frag_rows // 2, columns), jnp.bfloat16),
            pltpu.VMEM((frag_rows // 2, columns), jnp.float32),
            pltpu.VMEM((frag_rows // 4, columns), jnp.float32),
            pltpu.VMEM((ny - 1, frag_rows // (4 * ny), columns), jnp.float32),
            pltpu.VMEM((frag_rows, columns), jnp.float32),
            dma((CHUNKS,)), dma((W_PIECES,)), dma((W_PIECES,)), dma((nz - 1, 2, CHUNKS)), dma((nz - 2, CHUNKS)),
            dma((nz - 1, CHUNKS)), dma((TILES,)), dma((TILES // 2,)), dma((TILES // 2,)), dma((TILES,)),
            dma, dma, dma((2, 2)), dma((2, 2)), dma((TILES,)), dma((3,)), dma((2,)),
            dma, dma, dma, dma, dma((ny - 1,)), dma((ny - 1,)), dma((ny - 1,)), dma((ny - 1,)), dma, dma, dma, dma,
        ],
        cost_estimate=pl.CostEstimate(flops=flops, bytes_accessed=8 << 20, transcendentals=0),
        compiler_params=pltpu.CompilerParams(
            collective_id=0, has_side_effects=True, vmem_limit_bytes=59 << 20
        ),
    )(fragment, tokens, weight, anchor, momentum)


def local(nz, ny, params, anchor, momentum, tokens, fragment):
    params_out, momentum_out, anchor_out = window(
        nz, ny, fragment, tokens[0, 0], params[0], anchor, momentum
    )
    return (params_out[None], momentum_out, anchor_out)


def solution(mesh):
    return jax.shard_map(
        functools.partial(local, mesh.shape["tensor"] // 2, mesh.shape["replica"] // 4),
        mesh=mesh,
        in_specs=(
            P("replica", None, "tensor"),
            P(None, "tensor"),
            P(None, "tensor"),
            P("replica", None, "tensor", None),
            P(),
        ),
        out_specs=(P("replica", None, "tensor"), P(None, "tensor"), P(None, "tensor")),
        check_vma=False,
    )
```

```python
import functools
import math

import jax
import jax.numpy as jnp
from jax import lax
from jax.experimental import pallas as pl
from jax.experimental.pallas import tpu as pltpu
from jax.sharding import PartitionSpec as P

LATE_ROWS = 16
PARTS = (2, 2, 2, 1)
CHUNKS = len(PARTS)
W_PIECES = 8
TILES = 8

inner_rate = 128.0
outer_rate = 0.7
nesterov_mu = 0.9

MESH = pl.DeviceIdType.MESH


def step_kernel(
    nz, ny, total_rows, frag_ref, x_ref, w_ref, a_ref, m_ref, o_ref, mo_ref, ao_ref,
    xb, xq, wv, home, acc, resid, resid_late, stage, relay, back, fin,
    anchor, momentum, frag_out, frag_in, part, from_x, from_y, grad,
    own_send, w_send, w_recv, got, ring_send, sib_send, out_send, relay_recv, relay_send, back_recv,
    q_own, mate_send, mate_recv, q_send, q_recv, fin_sem, load_sem, store_sem,
    a_send, a_recv, b_send, b_recv, c_send, c_recv, d_send, d_recv, e_send, e_recv, f_send, f_recv,
):
    shard, width = x_ref.shape
    rows = shard - LATE_ROWS
    columns = w_ref.shape[1]
    sizes = [rows * part // 7 for part in PARTS]
    starts = [sum(sizes[:j]) for j in range(CHUNKS)]
    piece = width // W_PIECES
    tile = width // TILES
    inv_root = 1.0 / math.sqrt(width)

    rep = lax.axis_index("replica")
    ten = lax.axis_index("tensor")
    core = lax.rem(rep, 2)
    far = ten // nz
    z = lax.rem(ten, nz)
    up = (rep, far * nz + lax.rem(z + 1, nz))
    down = (rep, far * nz + lax.rem(z + nz - 1, nz))
    sibling = (rep + 1 - 2 * core, ten)
    partner = (rep + 1 - 2 * core, (1 - far) * nz + z)
    mate = (rep, (1 - far) * nz + z)
    ends = (
        (rep, far * nz + lax.rem(z + 1 - 2 * core + nz, nz)),
        (rep, far * nz + lax.rem(z - 1 + 2 * core + nz, nz)),
    )
    swapped = core + far == 1
    near = rep // (2 * ny)
    y = lax.rem(rep // 2, ny)
    across = (lax.rem(rep + 2 * ny, 4 * ny), ten)
    along = [((near * ny + lax.rem(y + d, ny)) * 2 + core, ten) for d in range(1, ny)]
    frag_rows = a_ref.shape[0]
    half_rows = frag_rows // 2
    quarter_rows = frag_rows // 4
    piece_rows = quarter_rows // ny
    half_first = core * half_rows
    quarter_first = half_first + near * quarter_rows
    piece_first = quarter_first + y * piece_rows
    col_first = pl.multiple_of((core * nz + z) * columns, columns)
    col_home = pl.multiple_of(ten * columns, columns)
    mine = core * rows
    other = (1 - core) * rows

    barrier = pltpu.get_barrier_semaphore()
    for peer in (up, down, sibling, mate, across, *along):
        pl.semaphore_signal(barrier, inc=1, device_id=peer, device_id_type=MESH)

    @pl.when(swapped)
    def _():
        pl.semaphore_signal(barrier, inc=1, device_id=partner, device_id_type=MESH)
        pl.semaphore_wait(barrier, 5 + ny)

    @pl.when(jnp.logical_not(swapped))
    def _():
        pl.semaphore_wait(barrier, 4 + ny)

    def remote(src, dst, send, recv, peer):
        return pltpu.make_async_remote_copy(
            src_ref=src, dst_ref=dst, send_sem=send, recv_sem=recv, device_id=peer, device_id_type=MESH
        )

    def x_over(j):
        return remote(
            x_ref.at[pl.ds(starts[j], sizes[j])], xb.at[0, pl.ds(other + starts[j], sizes[j])],
            own_send.at[j], got.at[0, 0, j], partner,
        )

    def w_over(k):
        return remote(
            w_ref.at[pl.ds(k * piece, piece)], wv.at[pl.ds(k * piece, piece)],
            w_send.at[k], w_recv.at[k], partner,
        )

    def x_here(j):
        return pltpu.make_async_copy(
            x_ref.at[pl.ds(starts[j], sizes[j])], xb.at[0, pl.ds(mine + starts[j], sizes[j])], got.at[0, 0, j]
        )

    def w_here(k):
        return pltpu.make_async_copy(
            w_ref.at[pl.ds(k * piece, piece)], wv.at[pl.ds(k * piece, piece)], w_recv.at[k]
        )

    late_src = x_ref.at[pl.ds(rows, LATE_ROWS)]

    def late_at(lane, step, way):
        offset = (nz - step) % nz if way == 0 else step
        return xq.at[pl.ds((lane * nz + offset) * LATE_ROWS, LATE_ROWS)]

    late_here = pltpu.make_async_copy(late_src, late_at(0, 0, 0), q_own)
    late_mate = remote(late_src, late_at(1, 0, 0), mate_send, mate_recv, mate)

    @pl.when(swapped)
    def _():
        for j in range(CHUNKS):
            x_over(j).start()

    late_here.start()
    late_mate.start()

    @pl.when(swapped)
    def _():
        for k in range(W_PIECES):
            w_over(k).start()

    @pl.when(jnp.logical_not(swapped))
    def _():
        for j in range(CHUNKS):
            x_here(j).start()
        for k in range(W_PIECES):
            w_here(k).start()

    loads = [
        pltpu.make_async_copy(src, dst, load_sem.at[k])
        for k, (src, dst) in enumerate(((w_ref, home), (a_ref, anchor), (m_ref, momentum)))
    ]
    for copy in loads:
        copy.start()

    def arrived(s, lane, j):
        place = (mine if lane == 0 else other) + starts[j]
        ref = xb.at[s, pl.ds(place, sizes[j])]
        pltpu.make_async_copy(ref, ref, got.at[s, lane, j]).wait()

    def ring(s, j):
        place = pl.ds(mine + starts[j], sizes[j])
        end = ends[0 if j in (0, CHUNKS - 1) else 1]
        return remote(xb.at[s, place], xb.at[s + 1, place], ring_send.at[s, j], got.at[s + 1, 0, j], end)

    def share(s, j):
        place = pl.ds(mine + starts[j], sizes[j])
        return remote(xb.at[s, place], xb.at[s, place], sib_send.at[s, j], got.at[s, 1, j], sibling)

    def pass_on(s, j, onward):
        arrived(s, 0, j)
        if onward:
            ring(s, j).start()
        share(s, j).start()

    def forward(s):
        for j in range(CHUNKS):
            arrived(s, 1, j)
        outputs = jnp.dot(xb[s], wv[...], preferred_element_type=jnp.float32) * inv_root
        target = xb[s, :, pl.ds(col_first, columns)].astype(jnp.float32)
        resid[...] = (outputs - target).astype(jnp.bfloat16)

    def grad_tile(s, t):
        return lax.dot_general(
            xb[s, :, pl.ds(t * tile, tile)], resid[...], (((0,), (0,)), ((), ())),
            preferred_element_type=jnp.float32,
        )

    def backward(s):
        @pl.loop(0, TILES)
        def _(t):
            t = pl.multiple_of(t * tile, tile)
            acc[pl.ds(t, tile), :] += lax.dot_general(
                xb[s, :, pl.ds(t, tile)], resid[...], (((0,), (0,)), ((), ())),
                preferred_element_type=jnp.float32,
            )

    over_core = remote(
        frag_out.at[pl.ds((1 - core) * half_rows, half_rows)], frag_in, a_send, a_recv, sibling
    )
    over_x = remote(
        part.at[pl.ds((1 - near) * quarter_rows, quarter_rows)], from_x, b_send, b_recv, across
    )
    over_y = [
        remote(
            part.at[pl.ds(near * quarter_rows + lax.rem(y + d, ny) * piece_rows, piece_rows)],
            from_y.at[d - 1], c_send.at[d - 1], c_recv.at[d - 1], along[d - 1],
        )
        for d in range(1, ny)
    ]
    piece_at = grad.at[pl.ds(piece_first, piece_rows)]
    quarter_at = grad.at[pl.ds(quarter_first, quarter_rows)]
    half_at = grad.at[pl.ds(half_first, half_rows)]
    back_y = [
        remote(piece_at, piece_at, d_send.at[d - 1], d_recv.at[d - 1], along[d - 1]) for d in range(1, ny)
    ]
    back_x = remote(quarter_at, quarter_at, e_send, e_recv, across)
    back_core = remote(half_at, half_at, f_send, f_recv, sibling)

    def chosen(k):
        return jnp.full((frag_rows, columns), frag_ref[0], jnp.int32) == k

    def sum_core():
        for copy in loads:
            copy.wait()
        rows_of = home[pl.ds(0, frag_rows), :].astype(jnp.float32)
        for k in range(1, width // frag_rows):
            block = home[pl.ds(k * frag_rows, frag_rows), :].astype(jnp.float32)
            rows_of = jnp.where(chosen(k), block, rows_of)
        frag_out[...] = rows_of.astype(jnp.bfloat16)
        over_core.start()

    def sum_x():
        over_core.wait()
        fixed = anchor[pl.ds(half_first, half_rows), :]
        own = frag_out[pl.ds(half_first, half_rows), :].astype(jnp.float32)
        part[...] = (fixed - own) + (fixed - frag_in[...].astype(jnp.float32))
        over_x.start()

    def sum_y():
        over_x.wait()
        part[pl.ds(near * quarter_rows, quarter_rows), :] += from_x[...]
        for copy in over_y:
            copy.start()

    def gather_y():
        for copy in over_y:
            copy.wait()
        total = part[pl.ds(near * quarter_rows + y * piece_rows, piece_rows), :]
        for d in range(1, ny):
            total += from_y[d - 1]
        grad[pl.ds(piece_first, piece_rows), :] = total / (4 * ny)
        for copy in back_y:
            copy.start()

    def gather_x():
        for copy in back_y:
            copy.wait()
        back_x.start()

    def gather_core():
        back_x.wait()
        back_core.start()

    stores = [
        pltpu.make_async_copy(src, dst, store_sem.at[k])
        for k, (src, dst) in enumerate(((momentum, mo_ref), (anchor, ao_ref)))
    ]

    def outer_step():
        back_core.wait()
        outer_grad = grad[...]
        moved = nesterov_mu * momentum[...] + outer_grad
        momentum[...] = moved
        anchor[...] = anchor[...] - outer_rate * (outer_grad + nesterov_mu * moved)
        for copy in stores:
            copy.start()

    def outer_stage(s):
        for k, stage_of in enumerate((sum_core, sum_x, sum_y, gather_y, gather_x, gather_core, outer_step)):
            pl.when(s == k)(stage_of)

    acc[...] = jnp.zeros_like(acc)
    half = nz // 2

    def early(s, carry):
        for j in range(CHUNKS):
            pass_on(s, j, True)
        outer_stage(s)
        return carry

    lax.fori_loop(0, half, early, 0)

    for k in range(W_PIECES):
        ref = wv.at[pl.ds(k * piece, piece)]
        pltpu.make_async_copy(ref, ref, w_recv.at[k]).wait()

    def late(s, carry):
        first = 2 * (s - half)
        pass_on(s, 0, True)
        forward(first)
        pass_on(s, 1, True)
        backward(first)
        pass_on(s, 2, True)
        forward(first + 1)
        pass_on(s, 3, True)
        backward(first + 1)
        outer_stage(s)
        return carry

    lax.fori_loop(half, nz - 1, late, 0)

    lanes = [(lane, way, half if lane == way else half - 1) for lane in range(2) for way in range(2)]

    def late_send(lane, step, way):
        return remote(
            late_at(lane, step - 1, way), late_at(lane, step, way),
            q_send.at[lane, way, step - 1], q_recv.at[lane, way, step - 1], (up, down)[way],
        )

    last = nz - 1
    pass_on(last, 0, False)
    forward(last - 1)
    pass_on(last, 1, False)
    backward(last - 1)
    pass_on(last, 2, False)
    pass_on(last, 3, False)
    late_here.wait()
    late_mate.wait()
    for lane, way, most in lanes:
        late_send(lane, 1, way).start()
    forward(last)

    def tile_at(t):
        return pl.ds(t * tile, tile)

    def relay_at(t):
        return relay.at[pl.ds(t // 2 * tile, tile)]

    def back_over(t):
        if t % 2 == 0:
            return remote(stage.at[tile_at(t)], back.at[tile_at(t)], out_send.at[t], back_recv.at[t], partner)
        return remote(stage.at[tile_at(t)], relay_at(t), out_send.at[t], relay_recv.at[t // 2], sibling)

    def back_relay(t):
        return remote(relay_at(t), back.at[tile_at(t)], relay_send.at[t // 2], back_recv.at[t], mate)

    @pl.when(swapped)
    def _():
        for t in range(TILES):
            stage[tile_at(t), :] = (acc[tile_at(t), :] + grad_tile(last, t)).astype(jnp.bfloat16)
            back_over(t).start()

    @pl.when(jnp.logical_not(swapped))
    def _():
        for t in range(TILES):
            acc[tile_at(t), :] += grad_tile(last, t)
            if t % 2 == 1:
                ref = relay_at(t)
                pltpu.make_async_copy(ref, ref, relay_recv.at[t // 2]).wait()
                back_relay(t).start()

    for step in range(1, half + 1):
        for lane, way, most in lanes:
            if step <= most:
                late_send(lane, step, way).wait_recv()
            if step < most:
                late_send(lane, step + 1, way).start()

    outputs = jnp.dot(xq[...], home[...], preferred_element_type=jnp.float32) * inv_root
    target = xq[:, pl.ds(col_home, columns)].astype(jnp.float32)
    resid_late[...] = (outputs - target).astype(jnp.bfloat16)

    def out_here(t):
        return pltpu.make_async_copy(fin.at[tile_at(t)], o_ref.at[tile_at(t)], fin_sem.at[t])

    for t in range(TILES):
        place = tile_at(t)

        @pl.when(swapped)
        def _():
            ref = back.at[place]
            pltpu.make_async_copy(ref, ref, back_recv.at[t]).wait()
            acc[place, :] = back[place, :].astype(jnp.float32)

        gradient = acc[place, :] + lax.dot_general(
            xq[:, place], resid_late[...], (((0,), (0,)), ((), ())), preferred_element_type=jnp.float32
        )
        scaled = gradient * (inv_root / total_rows)
        before = home[place, :].astype(jnp.float32)
        after = (before - inner_rate * scaled).astype(jnp.bfloat16).astype(jnp.float32)
        merged = anchor[...] + (after - before)
        fin[place, :] = jnp.where(chosen(t), merged, after).astype(jnp.bfloat16)
        out_here(t).start()

    @pl.when(swapped)
    def _():
        for j in range(CHUNKS):
            x_over(j).wait_send()
        for k in range(W_PIECES):
            w_over(k).wait_send()
        for t in range(TILES):
            back_over(t).wait_send()

    @pl.when(jnp.logical_not(swapped))
    def _():
        for t in range(1, TILES, 2):
            back_relay(t).wait_send()

    for lane, way, most in lanes:
        for step in range(1, most + 1):
            late_send(lane, step, way).wait_send()
    for t in range(TILES):
        out_here(t).wait()
    for copy in stores:
        copy.wait()

    def drain(s, carry):
        for j in range(CHUNKS):
            share(s, j).wait_send()
        return carry

    lax.fori_loop(0, nz, drain, 0)

    def drain_ring(s, carry):
        for j in range(CHUNKS):
            ring(s, j).wait_send()
        return carry

    lax.fori_loop(0, nz - 1, drain_ring, 0)


def window(nz, ny, fragment, tokens, weight, anchor, momentum):
    rows, width = tokens.shape
    columns = weight.shape[1]
    frag_rows = anchor.shape[0]
    total_rows = rows * 2 * nz
    flops = 4 * total_rows * width * columns
    whole = pl.BlockSpec(memory_space=pltpu.HBM)
    result = pl.BlockSpec(memory_space=pl.ANY)
    dma = pltpu.SemaphoreType.DMA
    return pl.pallas_call(
        functools.partial(step_kernel, nz, ny, total_rows),
        out_shape=(
            pltpu.VMEM((width, columns), jnp.bfloat16),
            pltpu.VMEM(momentum.shape, jnp.float32),
            pltpu.VMEM(anchor.shape, jnp.float32),
        ),
        in_specs=[pl.BlockSpec(memory_space=pltpu.SMEM), whole, whole, whole, whole],
        out_specs=(result, result, result),
        scratch_shapes=[
            pltpu.VMEM((nz, 2 * (rows - LATE_ROWS), width), jnp.bfloat16),
            pltpu.VMEM((2 * nz * LATE_ROWS, width), jnp.bfloat16),
            pltpu.VMEM((width, columns), jnp.bfloat16),
            pltpu.VMEM((width, columns), jnp.bfloat16),
            pltpu.VMEM((width, columns), jnp.float32),
            pltpu.VMEM((2 * (rows - LATE_ROWS), columns), jnp.bfloat16),
            pltpu.VMEM((2 * nz * LATE_ROWS, columns), jnp.bfloat16),
            pltpu.VMEM((width, columns), jnp.bfloat16),
            pltpu.VMEM((width // 2, columns), jnp.bfloat16),
            pltpu.VMEM((width, columns), jnp.bfloat16),
            pltpu.VMEM((width, columns), jnp.bfloat16),
            pltpu.VMEM((frag_rows, columns), jnp.float32),
            pltpu.VMEM((frag_rows, columns), jnp.float32),
            pltpu.VMEM((frag_rows, columns), jnp.bfloat16),
            pltpu.VMEM((frag_rows // 2, columns), jnp.bfloat16),
            pltpu.VMEM((frag_rows // 2, columns), jnp.float32),
            pltpu.VMEM((frag_rows // 4, columns), jnp.float32),
            pltpu.VMEM((ny - 1, frag_rows // (4 * ny), columns), jnp.float32),
            pltpu.VMEM((frag_rows, columns), jnp.float32),
            dma((CHUNKS,)), dma((W_PIECES,)), dma((W_PIECES,)), dma((nz, 2, CHUNKS)), dma((nz - 1, CHUNKS)),
            dma((nz, CHUNKS)), dma((TILES,)), dma((TILES // 2,)), dma((TILES // 2,)), dma((TILES,)),
            dma, dma, dma, dma((2, 2, nz // 2)), dma((2, 2, nz // 2)), dma((TILES,)), dma((3,)), dma((2,)),
            dma, dma, dma, dma, dma((ny - 1,)), dma((ny - 1,)), dma((ny - 1,)), dma((ny - 1,)), dma, dma, dma, dma,
        ],
        cost_estimate=pl.CostEstimate(flops=flops, bytes_accessed=8 << 20, transcendentals=0),
        compiler_params=pltpu.CompilerParams(
            collective_id=0, has_side_effects=True, vmem_limit_bytes=59 << 20
        ),
    )(fragment, tokens, weight, anchor, momentum)


def local(nz, ny, params, anchor, momentum, tokens, fragment):
    params_out, momentum_out, anchor_out = window(
        nz, ny, fragment, tokens[0, 0], params[0], anchor, momentum
    )
    return (params_out[None], momentum_out, anchor_out)


def solution(mesh):
    return jax.shard_map(
        functools.partial(local, mesh.shape["tensor"] // 2, mesh.shape["replica"] // 4),
        mesh=mesh,
        in_specs=(
            P("replica", None, "tensor"),
            P(None, "tensor"),
            P(None, "tensor"),
            P("replica", None, "tensor", None),
            P(),
        ),
        out_specs=(P("replica", None, "tensor"), P(None, "tensor"), P(None, "tensor")),
        check_vma=False,
    )
```
